32 devices in a mesh: dp: 8 (over z, x), ctx: 4 (over y, core).
Axes of the slice: x: 2, y: 2, z: 4, core: 2. Of those that a mesh axis runs over, the one named last changes fastest.
Arguments:
- tokens: bfloat16 [8, 2048, 768], P('dp', 'ctx'), may hold values from -6 to 6
- doc_ids: int32 [8, 2048], P('dp'), may hold values from 0 to 33, as said below
- pair_table: int32 [4], replicated, may hold values from 0 to 3, each once
- gain_attn: bfloat16 [768], P('dp'), may hold values from 0.5 to 1.5
- gain_ffn: bfloat16 [768], P('dp'), may hold values from 0.5 to 1.5
- w_qkv: bfloat16 [768, 2304], P('dp'), may hold values from -0.21875 to 0.21875
- w_out: bfloat16 [768, 768], P('dp'), may hold values from -2 to 2
- w_in: bfloat16 [768, 2304], P('dp'), may hold values from -0.21875 to 0.21875
- w_down: bfloat16 [1152, 768], P('dp'), may hold values from -0.1875 to 0.1875
- cotangent: bfloat16 [8, 2048, 768], P('dp', 'ctx'), may hold values from -6 to 6
Outputs:
- out_tokens: bfloat16 [8, 2048, 768], P('dp', 'ctx')
- grad_tokens: bfloat16 [8, 2048, 768], P('dp', 'ctx')
- grad_gain_attn: float32 [768], P('dp')
- grad_gain_ffn: float32 [768], P('dp')
- grad_w_qkv: float32 [768, 2304], P('dp')
- grad_w_out: float32 [768, 768], P('dp')
- grad_w_in: float32 [768, 2304], P('dp')
- grad_w_down: float32 [1152, 768], P('dp')
The draws below stay inside these ranges and needn't reach their ends.
Inputs may be any that keep to these rules, and one draw needn't show every extreme that they name: Along each sequence, in position order, doc_ids start at 0 and rise by 0 or 1 from one position to the next, and the last position of every sequence holds 33; one document of 1025 to 1536 tokens begins or ends each sequence. The device at index j along ctx holds blocks pair_table[j] and 7 - pair_table[j] of each of its sequences.
All inputs are finite; a program needn't handle non-finite values.
Results may differ from the reference program's by a relative error of at most 0.02.
Values may be sent and summed in bfloat16 or wider, within the bound.
A program may use at most 192 MiB of HBM per device.

```python
import math
import jax
import jax.numpy as jnp
from jax import lax

D = 768
HEADS = 12
HEAD_DIM = 64
FF = 1152
TOK_DEV = 512
SEQS = 8
LEN = 2048
NBLK = 8


def one_sequence(seq_key):
    length_key, side_key, mark_key = jax.random.split(seq_key, 3)
    longest = jax.random.randint(length_key, (), LEN // 2 + 1, 3 * LEN // 4 + 1)
    at_end = jax.random.randint(side_key, (), 0, 2)
    extra_starts = LEN // 64
    position = jnp.arange(LEN, dtype=jnp.int32)
    boundary = jnp.where(at_end == 1, LEN - longest, longest)
    in_rest = jnp.where(at_end == 1, position < boundary, position > boundary) & (position > 0)
    draws = jax.random.randint(mark_key, (LEN,), 0, 2 ** 30 // LEN)
    scores = jnp.where(in_rest, draws * LEN + position, -1)
    _, picked = lax_top(scores, extra_starts)
    chosen = jnp.zeros((LEN,), jnp.int32).at[picked].set(1)
    flags = jnp.where(position == boundary, 1, jnp.where(in_rest, chosen, 0))
    return jnp.cumsum(flags).astype(jnp.int32)


def lax_top(scores, count):
    return jax.lax.top_k(scores, count)


def draw_doc_ids(key, part):
    key = jax.random.fold_in(key, 7)
    seq_keys = jax.random.split(key, SEQS)
    return jax.vmap(one_sequence)(seq_keys)


def steps_of(stream_key, extent, cuts, smallest, high):
    def one(axis_at, blocks):
        steps = jax.random.uniform(jax.random.fold_in(jax.random.fold_in(stream_key, 6), axis_at), (blocks,), jnp.float32, smallest / len(cuts), high / len(cuts))
        return jnp.repeat(jnp.exp(steps), extent[axis_at] // blocks).reshape((-1,) + (1,) * (len(extent) - axis_at - 1))

    loudness = one(*cuts[0])
    for cut in cuts[1:]:
        loudness = loudness * one(*cut)
    return loudness


def noise(stream_key, extent, deviation, limit, shards=(), kind=jnp.bfloat16):
    drawn = deviation * jax.random.normal(stream_key, extent, jnp.float32)
    if shards:
        drawn = drawn * steps_of(stream_key, extent, shards, -0.22, 0.18)
    return jnp.clip(drawn, -limit, limit).astype(kind)


def setup_inputs(seed: int = 0) -> dict:
    arg_keys = jax.random.split(jax.random.key(seed), 11)
    return {
        "tokens": noise(arg_keys[0], (SEQS, LEN, D), 1.0, 6.0, ((0, 8), (1, 4))),
        "doc_ids": draw_doc_ids(jax.random.fold_in(arg_keys[10], 71), 0),
        "pair_table": jax.random.permutation(arg_keys[2], NBLK // 2).astype(jnp.int32),
        "gain_attn": jnp.clip(1.0 + 0.1 * jax.random.normal(arg_keys[3], (D,), jnp.float32), 0.5, 1.5).astype(jnp.bfloat16),
        "gain_ffn": jnp.clip(1.0 + 0.1 * jax.random.normal(arg_keys[4], (D,), jnp.float32), 0.5, 1.5).astype(jnp.bfloat16),
        "w_qkv": noise(arg_keys[5], (D, 3 * D), D ** -0.5, 0.21875, ((0, 8),)),
        "w_out": noise(arg_keys[6], (D, D), 8 ** -0.5, 2.0, ((0, 8),)),
        "w_in": noise(arg_keys[7], (D, 2 * FF), D ** -0.5, 0.21875, ((0, 8),)),
        "w_down": noise(arg_keys[8], (FF, D), FF ** -0.5, 0.1875, ((0, 8),)),
        "cotangent": noise(arg_keys[9], (SEQS, LEN, D), 1.0, 6.0, ((0, 8), (1, 4))),
    }


rope_base = 160000.0
norm_eps = 1e-05
masked_score = -1e+30

@jax.custom_vjp
def low(v):
    return lax.optimization_barrier(v.astype(jnp.bfloat16)).astype(jnp.float32)

@jax.custom_vjp
def low_back(v):
    return v

def low_keep(v):
    return (low(v), None)

def low_pass(kept, grad):
    return (grad,)

def back_keep(v):
    return (v, None)

def back_low(kept, grad):
    return (low(grad),)
low.defvjp(low_keep, low_pass)
low_back.defvjp(back_keep, back_low)

def layer_norm(inputs, scale_gain):
    centre = lax.optimization_barrier(jnp.mean(inputs, -1, keepdims=True))
    shifted = inputs - centre
    spread = lax.optimization_barrier(jnp.mean(shifted * shifted, -1, keepdims=True))
    return shifted * lax.rsqrt(spread + norm_eps) * scale_gain

def rotary(inputs, cosine_part, sine_part):
    half_dim = inputs.shape[-1] // 2
    leading = inputs[..., :half_dim]
    trailing = inputs[..., half_dim:]
    return jnp.concatenate([leading * cosine_part - trailing * sine_part, trailing * cosine_part + leading * sine_part], -1)

def rotary_tables(positions, head_dim):
    exponents = jnp.arange(head_dim // 2, dtype=jnp.float32) * (2.0 / head_dim)
    frequency = jnp.power(jnp.float32(rope_base), -exponents)
    angles = positions.astype(jnp.float32)[:, None] * frequency[None, :]
    return (jnp.cos(angles)[:, None, :], jnp.sin(angles)[:, None, :])

def dealt_positions(pair_table, rows_dev, ctx_size):
    half_rows = rows_dev // 2
    slot_index = jnp.arange(rows_dev * ctx_size, dtype=jnp.int32)
    owner_index = slot_index // rows_dev
    within = slot_index % rows_dev
    leading = jnp.take(pair_table, owner_index)
    block_index = jnp.where(within < half_rows, leading, 2 * ctx_size - 1 - leading)
    return (block_index * half_rows + within % half_rows).astype(jnp.int32)

def gated_gelu(gate_part, up_part):
    return jax.nn.gelu(gate_part, approximate=False) * up_part

def sequence_attention(queries, keys, values, positions, doc_slots):
    block_rows = min(LEN, 512)
    block_count = LEN // block_rows
    score_scale = 1.0 / math.sqrt(HEAD_DIM)

    def one_block(block_parts):
        query_part, query_pos, query_doc = block_parts
        scores = jnp.einsum('qhd,khd->hqk', query_part, keys, precision=lax.Precision.HIGHEST) * score_scale
        scores = low_back(scores)
        allowed = (doc_slots[None, :] == query_doc[:, None]) & (positions[None, :] <= query_pos[:, None])
        scores = jnp.where(allowed[None], scores, masked_score)
        row_top = lax.optimization_barrier(jnp.max(scores, -1, keepdims=True))
        shifted = jnp.exp(scores - row_top)
        probabilities = low(shifted / lax.optimization_barrier(jnp.sum(shifted, -1, keepdims=True)))
        return jnp.einsum('hqk,khd->qhd', probabilities, values, precision=lax.Precision.HIGHEST)
    saved_block = jax.checkpoint(one_block)
    result = lax.map(saved_block, (queries.reshape(block_count, block_rows, HEADS, HEAD_DIM), positions.reshape(block_count, block_rows), doc_slots.reshape(block_count, block_rows)))
    return result.reshape(LEN, HEADS * HEAD_DIM)

def layer_forward(x_rows, attn_scale, ffn_scale, qkv_weight, out_weight, in_weight, down_weight, positions, doc_slots):
    highest = lax.Precision.HIGHEST
    normed_attn = low(layer_norm(x_rows, attn_scale))
    qkv_rows = low_back(jnp.dot(normed_attn, qkv_weight, precision=highest, preferred_element_type=jnp.float32))
    shaped = qkv_rows.reshape(SEQS, LEN, 3, HEADS, HEAD_DIM)
    cosine_part, sine_part = rotary_tables(positions, HEAD_DIM)
    queries = low(rotary(shaped[:, :, 0], cosine_part, sine_part))
    keys = low(rotary(shaped[:, :, 1], cosine_part, sine_part))
    values = low(shaped[:, :, 2])

    def attend_sequence(sequence_parts):
        return sequence_attention(sequence_parts[0], sequence_parts[1], sequence_parts[2], positions, sequence_parts[3])
    attended = lax.map(attend_sequence, (queries, keys, values, doc_slots))
    attended = low(low_back(attended.reshape(SEQS * LEN, HEADS * HEAD_DIM)))
    mid_rows = x_rows + low_back(jnp.dot(attended, out_weight, precision=highest, preferred_element_type=jnp.float32))
    normed_ffn = low(layer_norm(mid_rows, ffn_scale))
    gate_up = low_back(jnp.dot(normed_ffn, in_weight, precision=highest, preferred_element_type=jnp.float32))
    mixed_low = low(gated_gelu(gate_up[:, :FF], gate_up[:, FF:]))
    return mid_rows + low_back(jnp.dot(mixed_low, down_weight, precision=highest, preferred_element_type=jnp.float32))

def reference(tokens, doc_ids, pair_table, gain_attn, gain_ffn, w_qkv, w_out, w_in, w_down, cotangent):
    positions = dealt_positions(pair_table, TOK_DEV, NBLK // 2)
    doc_slots = jnp.take(doc_ids, positions, axis=1)

    def run_layer(x_rows, attn_scale, ffn_scale, qkv_weight, out_weight, in_weight, down_weight):
        return layer_forward(x_rows, attn_scale, ffn_scale, qkv_weight, out_weight, in_weight, down_weight, positions, doc_slots)
    out_rows, pullback = jax.vjp(run_layer, tokens.reshape(SEQS * LEN, D).astype(jnp.float32), gain_attn.astype(jnp.float32), gain_ffn.astype(jnp.float32), w_qkv.astype(jnp.float32), w_out.astype(jnp.float32), w_in.astype(jnp.float32), w_down.astype(jnp.float32))
    grads = pullback(cotangent.reshape(SEQS * LEN, D).astype(jnp.float32))
    return (out_rows.reshape(SEQS, LEN, D).astype(jnp.bfloat16), grads[0].reshape(SEQS, LEN, D).astype(jnp.bfloat16), grads[1], grads[2], grads[3], grads[4], grads[5], grads[6])
```

```python
import math

import jax
import jax.numpy as jnp
from jax import lax
from jax.experimental import pallas as pl
from jax.experimental.pallas import tpu as pltpu
from jax.sharding import PartitionSpec as P

D = 768
HEADS = 12
HEAD_DIM = 64
FF = 1152
PAIRS = HEADS // 2
WIDE = 2 * HEAD_DIM

rope_base = 160000.0
norm_eps = 1e-05
masked_score = -1e30
score_scale = 1.0 / math.sqrt(HEAD_DIM)
vmem_bytes = 56 * 2**20


def contract(left, right, left_dim, right_dim):
    return lax.dot_general(
        left, right, (((left_dim,), (right_dim,)), ((), ())), preferred_element_type=jnp.float32
    )


def fill_bias(bias_ref, qpos_ref, qdoc_ref, kpos_ref, kdoc_ref, sub):
    def fill(block, carry):
        rows = pl.ds(pl.multiple_of(block * sub, sub), sub)
        ok = (kdoc_ref[rows, :] == qdoc_ref[...]) & (kpos_ref[rows, :] <= qpos_ref[...])
        bias_ref[rows, :] = jnp.where(ok, 0.0, masked_score)
        return carry

    lax.fori_loop(0, bias_ref.shape[0] // sub, fill, 0)


def both_heads(block):
    lane = lax.broadcasted_iota(jnp.int32, block.shape, 1)
    wide = block.astype(jnp.float32)
    return jnp.concatenate(
        [jnp.where(lane < HEAD_DIM, wide, 0.0), jnp.where(lane < HEAD_DIM, 0.0, wide)], 0
    ).astype(jnp.bfloat16)


def attend_kernel(
    seen_ref, q_ref, k_ref, v_ref, qpos_ref, qdoc_ref, kpos_ref, kdoc_ref,
    att_ref, lse_ref, bias_ref, top_ref, total_ref, acc_ref,
):
    sub = q_ref.shape[0] // 2
    blocks = k_ref.shape[0] // sub

    @pl.when(pl.program_id(0) == 0)
    def _():
        fill_bias(bias_ref, qpos_ref, qdoc_ref, kpos_ref, kdoc_ref, sub)

    for qb in range(2):
        own = slice(qb * sub, (qb + 1) * sub)
        queries = both_heads(q_ref[own, :])
        top_ref[...] = jnp.full(top_ref.shape, masked_score, jnp.float32)
        total_ref[...] = jnp.zeros(total_ref.shape, jnp.float32)
        acc_ref[...] = jnp.zeros(acc_ref.shape, jnp.float32)

        def step(kb, carry):
            @pl.when(seen_ref[qb * blocks + kb] != 0)
            def _():
                rows = pl.ds(pl.multiple_of(kb * sub, sub), sub)
                bias = bias_ref[rows, own]
                scores = contract(k_ref[rows, :], queries, 1, 1) + jnp.concatenate([bias, bias], 1)
                top = top_ref[...]
                new_top = jnp.maximum(top, jnp.max(scores, 0, keepdims=True))
                shrink = jnp.exp(top - new_top)
                weights = jnp.exp(scores - new_top)
                top_ref[...] = new_top
                total_ref[...] = total_ref[...] * shrink + jnp.sum(weights, 0, keepdims=True)
                acc_ref[...] = acc_ref[...] * shrink + contract(
                    v_ref[rows, :], weights.astype(jnp.bfloat16), 0, 0
                )

            return carry

        lax.fori_loop(0, blocks, step, 0)
        total = total_ref[...]
        scaled = acc_ref[...] / total
        turned = jnp.concatenate([scaled[:HEAD_DIM, :sub], scaled[HEAD_DIM:, sub:]], 0)
        att_ref[own, :] = turned.T
        lse_ref[0, qb : qb + 1, :] = top_ref[...] + jnp.log(total)


def pull_kernel(
    seen_ref, q_ref, k_ref, v_ref, datt_ref, att_ref, lse_ref,
    qpos_ref, qdoc_ref, kpos_ref, kdoc_ref,
    dq_ref, dkv_ref,
    bias_ref, queries_ref, datts_ref, delta_ref, dq_acc, dk_acc, dv_acc,
):
    sub = q_ref.shape[0] // 2
    blocks = k_ref.shape[0] // sub

    @pl.when(pl.program_id(0) == 0)
    def _():
        fill_bias(bias_ref, qpos_ref, qdoc_ref, kpos_ref, kdoc_ref, sub)

    for qb in range(2):
        own = slice(qb * sub, (qb + 1) * sub)
        queries_ref[qb] = both_heads(q_ref[own, :])
        datts_ref[qb] = both_heads(datt_ref[own, :])
        product = (datt_ref[own, :].astype(jnp.float32) * att_ref[own, :]).T
        delta_ref[qb : qb + 1, :] = jnp.concatenate(
            [
                jnp.sum(product[:HEAD_DIM], 0, keepdims=True),
                jnp.sum(product[HEAD_DIM:], 0, keepdims=True),
            ],
            1,
        )
    dq_acc[...] = jnp.zeros(dq_acc.shape, jnp.float32)

    def step(kb, carry):
        rows = pl.ds(pl.multiple_of(kb * sub, sub), sub)
        dk_acc[...] = jnp.zeros(dk_acc.shape, jnp.float32)
        dv_acc[...] = jnp.zeros(dv_acc.shape, jnp.float32)
        for qb in range(2):
            own = slice(qb * sub, (qb + 1) * sub)

            @pl.when(seen_ref[qb * blocks + kb] != 0)
            def _():
                keys = k_ref[rows, :]
                bias = bias_ref[rows, own]
                queries = queries_ref[qb]
                datts = datts_ref[qb]
                scores = contract(keys, queries, 1, 1) + jnp.concatenate([bias, bias], 1)
                weights = jnp.exp(scores - lse_ref[0, qb : qb + 1, :])
                d_weights = contract(v_ref[rows, :], datts, 1, 1)
                d_scores = (weights * (d_weights - delta_ref[qb : qb + 1, :])).astype(jnp.bfloat16)
                dv_acc[...] += contract(weights.astype(jnp.bfloat16), datts, 1, 0)
                dk_acc[...] += contract(d_scores, queries, 1, 0)
                dq_acc[qb] += contract(d_scores, keys, 0, 0)

        dkv_ref[0, rows, :] = dk_acc[...].astype(jnp.bfloat16)
        dkv_ref[1, rows, :] = dv_acc[...].astype(jnp.bfloat16)
        return carry

    lax.fori_loop(0, blocks, step, 0)
    lane = lax.broadcasted_iota(jnp.int32, (sub, WIDE), 1)
    for qb in range(2):
        own = slice(qb * sub, (qb + 1) * sub)
        dq_ref[own, :] = (
            jnp.where(lane < HEAD_DIM, dq_acc[qb, :sub, :], dq_acc[qb, sub:, :]) * score_scale
        )


def whole(shape):
    return pl.BlockSpec(shape, lambda pair: tuple(0 for _ in shape))


def per_pair(rows, first=0):
    return pl.BlockSpec((rows, WIDE), lambda pair: (0, first + pair))


def attend(seen, queries, kv, marks):
    rows, length = queries.shape[0], kv.shape[0]
    sub = rows // 2
    pairs = queries.shape[1] // WIDE
    return pl.pallas_call(
        attend_kernel,
        grid=(pairs,),
        in_specs=[
            pl.BlockSpec(memory_space=pltpu.SMEM),
            per_pair(rows), per_pair(length), per_pair(length, PAIRS),
            whole((1, rows)), whole((1, rows)), whole((length, 1)), whole((length, 1)),
        ],
        out_specs=[per_pair(rows), pl.BlockSpec((1, 2, rows), lambda pair: (pair, 0, 0))],
        out_shape=[
            jax.ShapeDtypeStruct((rows, queries.shape[1]), jnp.float32),
            jax.ShapeDtypeStruct((pairs, 2, rows), jnp.float32),
        ],
        scratch_shapes=[
            pltpu.VMEM((length, rows), jnp.float32),
            pltpu.VMEM((1, rows), jnp.float32),
            pltpu.VMEM((1, rows), jnp.float32),
            pltpu.VMEM((WIDE, rows), jnp.float32),
        ],
        compiler_params=pltpu.CompilerParams(vmem_limit_bytes=vmem_bytes),
        cost_estimate=pl.CostEstimate(
            flops=4 * rows * length * queries.shape[1], bytes_accessed=8 * length * D,
            transcendentals=rows * length * HEADS // 2,
        ),
    )(seen, queries, kv, kv, *marks)


def pull_attend(seen, queries, kv, d_att, att, log_total, marks):
    rows, length = queries.shape[0], kv.shape[0]
    sub = rows // 2
    pairs = queries.shape[1] // WIDE
    return pl.pallas_call(
        pull_kernel,
        grid=(pairs,),
        in_specs=[
            pl.BlockSpec(memory_space=pltpu.SMEM),
            per_pair(rows), per_pair(length), per_pair(length, PAIRS), per_pair(rows), per_pair(rows),
            pl.BlockSpec((1, 2, rows), lambda pair: (pair, 0, 0)),
            whole((1, rows)), whole((1, rows)), whole((length, 1)), whole((length, 1)),
        ],
        out_specs=[per_pair(rows), pl.BlockSpec((2, length, WIDE), lambda pair: (0, 0, pair))],
        out_shape=[
            jax.ShapeDtypeStruct((rows, queries.shape[1]), jnp.float32),
            jax.ShapeDtypeStruct((2, length, queries.shape[1]), jnp.bfloat16),
        ],
        scratch_shapes=[
            pltpu.VMEM((length, rows), jnp.float32),
            pltpu.VMEM((2, rows, WIDE), jnp.bfloat16),
            pltpu.VMEM((2, rows, WIDE), jnp.bfloat16),
            pltpu.VMEM((2, rows), jnp.float32),
            pltpu.VMEM((2, rows, WIDE), jnp.float32),
            pltpu.VMEM((sub, WIDE), jnp.float32),
            pltpu.VMEM((sub, WIDE), jnp.float32),
        ],
        compiler_params=pltpu.CompilerParams(vmem_limit_bytes=vmem_bytes),
        cost_estimate=pl.CostEstimate(
            flops=10 * rows * length * queries.shape[1], bytes_accessed=12 * length * D,
            transcendentals=rows * length * HEADS // 2,
        ),
    )(seen, queries, kv, kv, d_att, att, log_total, *marks)


def layer_norm(inputs, scale_gain):
    centre = jnp.mean(inputs, -1, keepdims=True)
    shifted = inputs - centre
    spread = jnp.mean(shifted * shifted, -1, keepdims=True)
    return shifted * lax.rsqrt(spread + norm_eps) * scale_gain


def rotary_tables(positions):
    exponents = jnp.arange(HEAD_DIM // 2, dtype=jnp.float32) * (2.0 / HEAD_DIM)
    frequency = jnp.power(jnp.float32(rope_base), -exponents)
    angles = positions.astype(jnp.float32)[:, None] * frequency[None, :]
    cosine, sine = jnp.cos(angles), jnp.sin(angles)
    return (
        jnp.tile(jnp.concatenate([cosine, cosine], 1), (1, HEADS)),
        jnp.tile(jnp.concatenate([-sine, sine], 1), (1, HEADS)),
    )


def rotary(inputs, cosine, signed_sine):
    half = HEAD_DIM // 2
    lane = lax.broadcasted_iota(jnp.int32, inputs.shape, 1) % HEAD_DIM
    swapped = jnp.where(lane < half, jnp.roll(inputs, -half, 1), jnp.roll(inputs, half, 1))
    return inputs * cosine + swapped * signed_sine


def gated_gelu(gate_part, up_part):
    return jax.nn.gelu(gate_part, approximate=False) * up_part


def bits_down(axis):
    count = (lax.axis_size(axis) - 1).bit_length()
    return [(axis, 1 << i) for i in reversed(range(count))]


def swap(array, axis, bit):
    count = lax.axis_size(axis)
    return lax.ppermute(array, axis, [(i, i ^ bit) for i in range(count)])


def bit_here(step):
    return (lax.axis_index(step[0]) // step[1]) % 2


def halve(array, place, step):
    here = bit_here(step)
    kept = lax.dynamic_index_in_dim(array, here, place, True)
    got = swap(lax.dynamic_index_in_dim(array, 1 - here, place, True), *step)
    return (kept.astype(jnp.float32) + got.astype(jnp.float32)).astype(jnp.bfloat16)


def double(array, place, step):
    got = swap(array, *step)
    return jnp.where(
        bit_here(step) == 0,
        jnp.concatenate([array, got], place),
        jnp.concatenate([got, array], place),
    )


def gather(array, places, order):
    array = array.reshape((1,) * len(places) + array.shape)
    for step in order:
        array = double(array, places.index(step), step)
    return array


def gather_rows(array, order):
    ctx_used = [step for step in bits_down("ctx") if step in order]
    share = 0
    for step in ctx_used:
        share = share * 2 + bit_here(step)
    rows = array.shape[0] // 2 ** len(ctx_used)
    part = lax.dynamic_slice_in_dim(array, share * rows, rows)
    return gather(part, bits_down("dp") + ctx_used, order).reshape(-1, array.shape[1])


def owned_sums(parts, order):
    ctx = lax.axis_size("ctx")
    counts = [part.shape[1] for part in parts]
    missing = -sum(counts) % (8 * ctx)
    if missing:
        last = jnp.pad(parts[-1], ((0, 0), (0, missing), (0, 0)))
        parts = parts[:-1] + [last]
    packed = jnp.concatenate(parts, 1) if len(parts) > 1 else parts[0]
    total = packed.shape[1]
    places = bits_down("dp") + bits_down("ctx")
    packed = packed.reshape((2,) * len(places) + (total // ctx, D))
    for step in order:
        packed = halve(packed, places.index(step), step)
    for step in bits_down("ctx"):
        packed = double(packed, places.index(step), step)
    full = packed.reshape(total, D).astype(jnp.float32)
    found, start = [], 0
    for count in counts:
        found.append(full[start : start + count])
        start += count
    return found


def by_owner(array):
    dp = lax.axis_size("dp")
    return array.astype(jnp.bfloat16).reshape(dp, array.shape[0] // dp, D)


def gain_row(array):
    dp = lax.axis_size("dp")
    rows = array.astype(jnp.bfloat16).reshape(dp, 1, D // dp)
    return jnp.pad(rows, ((0, 0), (0, 0), (0, D - D // dp)))


def on_device(
    tokens, doc_ids, pair_table, gain_attn, gain_ffn, w_qkv, w_out, w_in, w_down, cotangent
):
    dp_size, ctx_size = lax.axis_size("dp"), lax.axis_size("ctx")
    ctx_here = lax.axis_index("ctx")
    rows_dev = tokens.shape[1]
    sub = rows_dev // 2
    seq_len = rows_dev * ctx_size
    blocks = 2 * ctx_size
    pair = pair_table.astype(jnp.int32)
    block_ids = jnp.stack([pair, blocks - 1 - pair], 1).reshape(blocks)
    positions = (
        block_ids[:, None] * sub + jnp.arange(sub, dtype=jnp.int32)[None, :]
    ).reshape(seq_len)
    doc_slots = jnp.take(doc_ids[0].reshape(blocks, sub), block_ids, axis=0).reshape(seq_len)
    pos_own = lax.dynamic_slice_in_dim(positions, ctx_here * rows_dev, rows_dev)
    doc_own = lax.dynamic_slice_in_dim(doc_slots, ctx_here * rows_dev, rows_dev)
    ids_own = lax.dynamic_slice_in_dim(block_ids, ctx_here * 2, 2)
    low_doc = doc_slots.reshape(blocks, sub)[:, 0]
    high_doc = doc_slots.reshape(blocks, sub)[:, -1]
    low_own = doc_own.reshape(2, sub)[:, 0]
    seen = (
        ((block_ids[None, :] <= ids_own[:, None]) & (high_doc[None, :] >= low_own[:, None]))
        .astype(jnp.int32)
        .reshape(2 * blocks)
    )
    marks = (
        pos_own.reshape(1, rows_dev), doc_own.reshape(1, rows_dev),
        positions.reshape(seq_len, 1), doc_slots.reshape(seq_len, 1),
    )
    cosine, sine = rotary_tables(pos_own)

    dp_bits, ctx_bits = bits_down("dp"), bits_down("ctx")
    core, far = ctx_bits[-1:], ctx_bits[:-1]
    near_x, along_z = dp_bits[-1:], dp_bits[:-1]
    kv_full = gather_rows(w_qkv[:, D:], dp_bits + ctx_bits)
    share = D // dp_size // ctx_size
    gains_here = jnp.pad(
        jnp.stack([gain_attn, gain_ffn]), ((0, 6), (0, D - D // dp_size))
    )
    q_part = jnp.concatenate(
        [lax.dynamic_slice_in_dim(w_qkv[:, :D], ctx_here * share, share), gains_here], 0
    )
    q_packed = gather(q_part, dp_bits + ctx_bits, along_z + far + near_x + core)
    q_packed = q_packed.reshape(dp_size, ctx_size, share + 8, D)
    q_full = q_packed[:, :, :share].reshape(D, D)
    gains = q_packed[:, 0, share : share + 2, : D // dp_size].astype(jnp.float32)
    gains = gains.transpose(1, 0, 2).reshape(2, D)
    in_full = gather_rows(w_in, dp_bits + core)
    out_rows_here = w_out.shape[0]
    tail = gather_rows(jnp.concatenate([w_out, w_down], 0), dp_bits + core)
    tail = tail.reshape(dp_size, -1, D)
    out_full = tail[:, :out_rows_here].reshape(D, D)
    down_full = tail[:, out_rows_here:].reshape(FF, D)
    x_rows = tokens[0].astype(jnp.float32)
    normed_attn, pull_attn = jax.vjp(layer_norm, x_rows, gains[0])
    normed_low = normed_attn.astype(jnp.bfloat16)
    kv_rows = jnp.dot(normed_low, kv_full, preferred_element_type=jnp.float32)
    keys_own = rotary(kv_rows[:, :D], cosine, sine).astype(jnp.bfloat16)
    kv_own = jnp.concatenate([keys_own, kv_rows[:, D:].astype(jnp.bfloat16)], 1)
    kv_all = gather(kv_own, ctx_bits, ctx_bits).reshape(seq_len, 2 * D)
    q_rows = jnp.dot(normed_low, q_full, preferred_element_type=jnp.float32)
    queries = (rotary(q_rows, cosine, sine) * score_scale).astype(jnp.bfloat16)
    attended_sum, log_total = attend(seen, queries, kv_all, marks)
    attended = attended_sum.astype(jnp.bfloat16)
    mid_rows = x_rows + jnp.dot(attended, out_full, preferred_element_type=jnp.float32)
    normed_ffn, pull_ffn = jax.vjp(layer_norm, mid_rows, gains[1])
    normed_second = normed_ffn.astype(jnp.bfloat16)
    gate_up = jnp.dot(normed_second, in_full, preferred_element_type=jnp.float32)
    mixed_float, pull_mix = jax.vjp(gated_gelu, gate_up[:, :FF], gate_up[:, FF:])
    mixed_low = mixed_float.astype(jnp.bfloat16)
    d_out_low = cotangent[0]
    d_mixed = contract(d_out_low, down_full, 1, 1)
    d_gate, d_up = pull_mix(d_mixed)
    d_gate_up = jnp.concatenate([d_gate, d_up], 1).astype(jnp.bfloat16)
    d_normed_second = contract(d_gate_up, in_full, 1, 1)
    d_mid_norm, grad_ffn_gain = pull_ffn(d_normed_second)
    d_mid = d_out_low.astype(jnp.float32) + d_mid_norm
    d_branch = d_mid.astype(jnp.bfloat16)
    grad_down = contract(mixed_low, d_out_low, 0, 0)
    grad_in = [contract(normed_second, d_gate_up[:, i * D : (i + 1) * D], 0, 0) for i in range(3)]
    grad_out = contract(attended, d_branch, 0, 0)
    in_sums = owned_sums(
        [by_owner(part) for part in grad_in], core + near_x + along_z[::-1] + far
    )
    tail_sums = owned_sums(
        [by_owner(grad_down), by_owner(grad_out), gain_row(grad_ffn_gain)],
        core + far + near_x + along_z[::-1],
    )
    d_att = contract(d_branch, out_full, 1, 1).astype(jnp.bfloat16)
    d_queries, d_kv_all = pull_attend(seen, queries, kv_all, d_att, attended_sum, log_total, marks)
    out_rows = mid_rows + jnp.dot(mixed_low, down_full, preferred_element_type=jnp.float32)
    d_kv = d_kv_all.reshape((2,) + (2,) * len(ctx_bits) + (rows_dev, D))
    for step in core + far:
        d_kv = halve(d_kv, 1 + ctx_bits.index(step), step)
    d_kv = d_kv.reshape(2, rows_dev, D)
    d_q = rotary(d_queries, cosine, -sine).astype(jnp.bfloat16)
    q_sums = owned_sums(
        [by_owner(contract(normed_low, d_q, 0, 0))], core + near_x + far + along_z[::-1]
    )
    d_v = d_kv[1]
    v_sums = owned_sums(
        [by_owner(contract(normed_low, d_v, 0, 0))], core + near_x + far + along_z[::-1]
    )
    d_k = rotary(d_kv[0].astype(jnp.float32), cosine, -sine).astype(jnp.bfloat16)
    d_normed_attn = contract(d_q, q_full, 1, 1) + contract(
        jnp.concatenate([d_k, d_v], 1), kv_full, 1, 1
    )
    d_x_norm, grad_attn_gain = pull_attn(d_normed_attn)
    grad_rows = (d_mid + d_x_norm).astype(jnp.bfloat16)
    k_sums = owned_sums(
        [by_owner(contract(normed_low, d_k, 0, 0)), gain_row(grad_attn_gain)],
        core + far + near_x + along_z[::-1],
    )
    return (
        out_rows.astype(jnp.bfloat16)[None],
        grad_rows[None],
        k_sums[1][0, : D // dp_size],
        tail_sums[2][0, : D // dp_size],
        jnp.concatenate([q_sums[0], k_sums[0], v_sums[0]], 1),
        tail_sums[1],
        jnp.concatenate(in_sums, 1),
        tail_sums[0],
    )


def solution(mesh):
    return jax.shard_map(
        on_device,
        mesh=mesh,
        in_specs=(
            P("dp", "ctx", None),
            P("dp", None),
            P(),
            P("dp"),
            P("dp"),
            P("dp", None),
            P("dp", None),
            P("dp", None),
            P("dp", None),
            P("dp", "ctx", None),
        ),
        out_specs=(
            P("dp", "ctx", None),
            P("dp", "ctx", None),
            P("dp"),
            P("dp"),
            P("dp", None),
            P("dp", None),
            P("dp", None),
            P("dp", None),
        ),
        check_vma=False,
    )
```

```python
import math

import jax
import jax.numpy as jnp
from jax import lax
from jax.experimental import pallas as pl
from jax.experimental.pallas import tpu as pltpu
from jax.sharding import PartitionSpec as P

D = 768
HEADS = 12
HEAD_DIM = 64
FF = 1152
PAIRS = HEADS // 2
WIDE = 2 * HEAD_DIM

rope_base = 160000.0
norm_eps = 1e-05
masked_score = -1e30
score_scale = 1.0 / math.sqrt(HEAD_DIM)
vmem_bytes = 56 * 2**20


def contract(left, right, left_dim, right_dim):
    return lax.dot_general(
        left, right, (((left_dim,), (right_dim,)), ((), ())), preferred_element_type=jnp.float32
    )


def fill_bias(bias_ref, qpos_ref, qdoc_ref, kpos_ref, kdoc_ref, sub):
    def fill(block, carry):
        rows = pl.ds(pl.multiple_of(block * sub, sub), sub)
        ok = (kdoc_ref[rows, :] == qdoc_ref[...]) & (kpos_ref[rows, :] <= qpos_ref[...])
        bias_ref[rows, :] = jnp.where(ok, 0.0, masked_score)
        return carry

    lax.fori_loop(0, bias_ref.shape[0] // sub, fill, 0)


def both_heads(block):
    lane = lax.broadcasted_iota(jnp.int32, block.shape, 1)
    wide = block.astype(jnp.float32)
    return jnp.concatenate(
        [jnp.where(lane < HEAD_DIM, wide, 0.0), jnp.where(lane < HEAD_DIM, 0.0, wide)], 0
    ).astype(jnp.bfloat16)


def attend_kernel(
    seen_ref, q_ref, k_ref, v_ref, qpos_ref, qdoc_ref, kpos_ref, kdoc_ref,
    att_ref, lse_ref, bias_ref, top_ref, total_ref, acc_ref,
):
    sub = q_ref.shape[0] // 2
    blocks = k_ref.shape[0] // sub

    @pl.when(pl.program_id(0) == 0)
    def _():
        fill_bias(bias_ref, qpos_ref, qdoc_ref, kpos_ref, kdoc_ref, sub)

    for qb in range(2):
        own = slice(qb * sub, (qb + 1) * sub)
        queries = both_heads(q_ref[own, :])
        top_ref[...] = jnp.full(top_ref.shape, masked_score, jnp.float32)
        total_ref[...] = jnp.zeros(total_ref.shape, jnp.float32)
        acc_ref[...] = jnp.zeros(acc_ref.shape, jnp.float32)

        def step(kb, carry):
            @pl.when(seen_ref[qb * blocks + kb] != 0)
            def _():
                rows = pl.ds(pl.multiple_of(kb * sub, sub), sub)
                bias = bias_ref[rows, own]
                scores = contract(k_ref[rows, :], queries, 1, 1) + jnp.concatenate([bias, bias], 1)
                top = top_ref[...]
                new_top = jnp.maximum(top, jnp.max(scores, 0, keepdims=True))
                shrink = jnp.exp(top - new_top)
                weights = jnp.exp(scores - new_top)
                top_ref[...] = new_top
                total_ref[...] = total_ref[...] * shrink + jnp.sum(weights, 0, keepdims=True)
                acc_ref[...] = acc_ref[...] * shrink + contract(
                    v_ref[rows, :], weights.astype(jnp.bfloat16), 0, 0
                )

            return carry

        lax.fori_loop(0, blocks, step, 0)
        total = total_ref[...]
        scaled = acc_ref[...] / total
        turned = jnp.concatenate([scaled[:HEAD_DIM, :sub], scaled[HEAD_DIM:, sub:]], 0)
        att_ref[own, :] = turned.T
        lse_ref[0, qb : qb + 1, :] = top_ref[...] + jnp.log(total)


def pull_kernel(
    seen_ref, q_ref, k_ref, v_ref, datt_ref, att_ref, lse_ref,
    qpos_ref, qdoc_ref, kpos_ref, kdoc_ref,
    dq_ref, dkv_ref,
    bias_ref, queries_ref, datts_ref, delta_ref, dq_acc, dk_acc, dv_acc,
):
    sub = q_ref.shape[0] // 2
    blocks = k_ref.shape[0] // sub

    @pl.when(pl.program_id(0) == 0)
    def _():
        fill_bias(bias_ref, qpos_ref, qdoc_ref, kpos_ref, kdoc_ref, sub)

    for qb in range(2):
        own = slice(qb * sub, (qb + 1) * sub)
        queries_ref[qb] = both_heads(q_ref[own, :])
        datts_ref[qb] = both_heads(datt_ref[own, :])
        product = (datt_ref[own, :].astype(jnp.float32) * att_ref[own, :]).T
        delta_ref[qb : qb + 1, :] = jnp.concatenate(
            [
                jnp.sum(product[:HEAD_DIM], 0, keepdims=True),
                jnp.sum(product[HEAD_DIM:], 0, keepdims=True),
            ],
            1,
        )
    dq_acc[...] = jnp.zeros(dq_acc.shape, jnp.float32)

    def step(kb, carry):
        rows = pl.ds(pl.multiple_of(kb * sub, sub), sub)
        dk_acc[...] = jnp.zeros(dk_acc.shape, jnp.float32)
        dv_acc[...] = jnp.zeros(dv_acc.shape, jnp.float32)
        for qb in range(2):
            own = slice(qb * sub, (qb + 1) * sub)

            @pl.when(seen_ref[qb * blocks + kb] != 0)
            def _():
                keys = k_ref[rows, :]
                bias = bias_ref[rows, own]
                queries = queries_ref[qb]
                datts = datts_ref[qb]
                scores = contract(keys, queries, 1, 1) + jnp.concatenate([bias, bias], 1)
                weights = jnp.exp(scores - lse_ref[0, qb : qb + 1, :])
                d_weights = contract(v_ref[rows, :], datts, 1, 1)
                d_scores = (weights * (d_weights - delta_ref[qb : qb + 1, :])).astype(jnp.bfloat16)
                dv_acc[...] += contract(weights.astype(jnp.bfloat16), datts, 1, 0)
                dk_acc[...] += contract(d_scores, queries, 1, 0)
                dq_acc[qb] += contract(d_scores, keys, 0, 0)

        dkv_ref[0, rows, :] = dk_acc[...].astype(jnp.bfloat16)
        dkv_ref[1, rows, :] = dv_acc[...].astype(jnp.bfloat16)
        return carry

    lax.fori_loop(0, blocks, step, 0)
    lane = lax.broadcasted_iota(jnp.int32, (sub, WIDE), 1)
    for qb in range(2):
        own = slice(qb * sub, (qb + 1) * sub)
        dq_ref[own, :] = (
            jnp.where(lane < HEAD_DIM, dq_acc[qb, :sub, :], dq_acc[qb, sub:, :]) * score_scale
        )


def whole(shape):
    return pl.BlockSpec(shape, lambda pair: tuple(0 for _ in shape))


def per_pair(rows, first=0):
    return pl.BlockSpec((rows, WIDE), lambda pair: (0, first + pair))


def attend(seen, queries, kv, marks):
    rows, length = queries.shape[0], kv.shape[0]
    sub = rows // 2
    pairs = queries.shape[1] // WIDE
    return pl.pallas_call(
        attend_kernel,
        grid=(pairs,),
        in_specs=[
            pl.BlockSpec(memory_space=pltpu.SMEM),
            per_pair(rows), per_pair(length), per_pair(length, PAIRS),
            whole((1, rows)), whole((1, rows)), whole((length, 1)), whole((length, 1)),
        ],
        out_specs=[per_pair(rows), pl.BlockSpec((1, 2, rows), lambda pair: (pair, 0, 0))],
        out_shape=[
            jax.ShapeDtypeStruct((rows, queries.shape[1]), jnp.float32),
            jax.ShapeDtypeStruct((pairs, 2, rows), jnp.float32),
        ],
        scratch_shapes=[
            pltpu.VMEM((length, rows), jnp.float32),
            pltpu.VMEM((1, rows), jnp.float32),
            pltpu.VMEM((1, rows), jnp.float32),
            pltpu.VMEM((WIDE, rows), jnp.float32),
        ],
        compiler_params=pltpu.CompilerParams(vmem_limit_bytes=vmem_bytes),
        cost_estimate=pl.CostEstimate(
            flops=4 * rows * length * queries.shape[1], bytes_accessed=8 * length * D,
            transcendentals=rows * length * HEADS // 2,
        ),
    )(seen, queries, kv, kv, *marks)


def pull_attend(seen, queries, kv, d_att, att, log_total, marks):
    rows, length = queries.shape[0], kv.shape[0]
    sub = rows // 2
    pairs = queries.shape[1] // WIDE
    return pl.pallas_call(
        pull_kernel,
        grid=(pairs,),
        in_specs=[
            pl.BlockSpec(memory_space=pltpu.SMEM),
            per_pair(rows), per_pair(length), per_pair(length, PAIRS), per_pair(rows), per_pair(rows),
            pl.BlockSpec((1, 2, rows), lambda pair: (pair, 0, 0)),
            whole((1, rows)), whole((1, rows)), whole((length, 1)), whole((length, 1)),
        ],
        out_specs=[per_pair(rows), pl.BlockSpec((2, length, WIDE), lambda pair: (0, 0, pair))],
        out_shape=[
            jax.ShapeDtypeStruct((rows, queries.shape[1]), jnp.float32),
            jax.ShapeDtypeStruct((2, length, queries.shape[1]), jnp.bfloat16),
        ],
        scratch_shapes=[
            pltpu.VMEM((length, rows), jnp.float32),
            pltpu.VMEM((2, rows, WIDE), jnp.bfloat16),
            pltpu.VMEM((2, rows, WIDE), jnp.bfloat16),
            pltpu.VMEM((2, rows), jnp.float32),
            pltpu.VMEM((2, rows, WIDE), jnp.float32),
            pltpu.VMEM((sub, WIDE), jnp.float32),
            pltpu.VMEM((sub, WIDE), jnp.float32),
        ],
        compiler_params=pltpu.CompilerParams(vmem_limit_bytes=vmem_bytes),
        cost_estimate=pl.CostEstimate(
            flops=10 * rows * length * queries.shape[1], bytes_accessed=12 * length * D,
            transcendentals=rows * length * HEADS // 2,
        ),
    )(seen, queries, kv, kv, d_att, att, log_total, *marks)


def layer_norm(inputs, scale_gain):
    centre = jnp.mean(inputs, -1, keepdims=True)
    shifted = inputs - centre
    spread = jnp.mean(shifted * shifted, -1, keepdims=True)
    return shifted * lax.rsqrt(spread + norm_eps) * scale_gain


def rotary_tables(positions):
    exponents = jnp.arange(HEAD_DIM // 2, dtype=jnp.float32) * (2.0 / HEAD_DIM)
    frequency = jnp.power(jnp.float32(rope_base), -exponents)
    angles = positions.astype(jnp.float32)[:, None] * frequency[None, :]
    cosine, sine = jnp.cos(angles), jnp.sin(angles)
    return (
        jnp.tile(jnp.concatenate([cosine, cosine], 1), (1, HEADS)),
        jnp.tile(jnp.concatenate([-sine, sine], 1), (1, HEADS)),
    )


def rotary(inputs, cosine, signed_sine):
    half = HEAD_DIM // 2
    lane = lax.broadcasted_iota(jnp.int32, inputs.shape, 1) % HEAD_DIM
    swapped = jnp.where(lane < half, jnp.roll(inputs, -half, 1), jnp.roll(inputs, half, 1))
    return inputs * cosine + swapped * signed_sine


def gated_gelu(gate_part, up_part):
    return jax.nn.gelu(gate_part, approximate=False) * up_part


def bits_down(axis):
    count = (lax.axis_size(axis) - 1).bit_length()
    return [(axis, 1 << i) for i in reversed(range(count))]


def swap(array, axis, bit):
    count = lax.axis_size(axis)
    return lax.ppermute(array, axis, [(i, i ^ bit) for i in range(count)])


def bit_here(step):
    return (lax.axis_index(step[0]) // step[1]) % 2


def halve(array, place, step):
    here = bit_here(step)
    kept = lax.dynamic_index_in_dim(array, here, place, True)
    got = swap(lax.dynamic_index_in_dim(array, 1 - here, place, True), *step)
    return (kept.astype(jnp.float32) + got.astype(jnp.float32)).astype(jnp.bfloat16)


def double(array, place, step):
    got = swap(array, *step)
    return jnp.where(
        bit_here(step) == 0,
        jnp.concatenate([array, got], place),
        jnp.concatenate([got, array], place),
    )


def gather(array, places, order):
    array = array.reshape((1,) * len(places) + array.shape)
    for step in order:
        array = double(array, places.index(step), step)
    return array


def gather_rows(array, order):
    ctx_used = [step for step in bits_down("ctx") if step in order]
    share = 0
    for step in ctx_used:
        share = share * 2 + bit_here(step)
    rows = array.shape[0] // 2 ** len(ctx_used)
    part = lax.dynamic_slice_in_dim(array, share * rows, rows)
    return gather(part, bits_down("dp") + ctx_used, order).reshape(-1, array.shape[1])


def pack_parts(parts):
    ctx = lax.axis_size("ctx")
    missing = -sum(part.shape[1] for part in parts) % (8 * ctx)
    if missing:
        last = jnp.pad(parts[-1], ((0, 0), (0, missing), (0, 0)))
        parts = parts[:-1] + [last]
    packed = jnp.concatenate(parts, 1) if len(parts) > 1 else parts[0]
    bits = len(bits_down("dp") + bits_down("ctx"))
    return packed.reshape((2,) * bits + (packed.shape[1] // ctx, D))


def halve_all(packed, order):
    places = bits_down("dp") + bits_down("ctx")
    for step in order:
        packed = halve(packed, places.index(step), step)
    return packed


def unpack_sums(packed, counts):
    places = bits_down("dp") + bits_down("ctx")
    for step in bits_down("ctx"):
        packed = double(packed, places.index(step), step)
    full = packed.reshape(-1, D).astype(jnp.float32)
    found, start = [], 0
    for count in counts:
        found.append(full[start : start + count])
        start += count
    return found


def owned_sums(parts, order):
    counts = [part.shape[1] for part in parts]
    return unpack_sums(halve_all(pack_parts(parts), order), counts)


def by_owner(array):
    dp = lax.axis_size("dp")
    return array.astype(jnp.bfloat16).reshape(dp, array.shape[0] // dp, D)


def gain_row(array):
    dp = lax.axis_size("dp")
    rows = array.astype(jnp.bfloat16).reshape(dp, 1, D // dp)
    return jnp.pad(rows, ((0, 0), (0, 0), (0, D - D // dp)))


def on_device(
    tokens, doc_ids, pair_table, gain_attn, gain_ffn, w_qkv, w_out, w_in, w_down, cotangent
):
    dp_size, ctx_size = lax.axis_size("dp"), lax.axis_size("ctx")
    ctx_here = lax.axis_index("ctx")
    rows_dev = tokens.shape[1]
    sub = rows_dev // 2
    seq_len = rows_dev * ctx_size
    blocks = 2 * ctx_size
    pair = pair_table.astype(jnp.int32)
    block_ids = jnp.stack([pair, blocks - 1 - pair], 1).reshape(blocks)
    positions = (
        block_ids[:, None] * sub + jnp.arange(sub, dtype=jnp.int32)[None, :]
    ).reshape(seq_len)
    doc_slots = jnp.take(doc_ids[0].reshape(blocks, sub), block_ids, axis=0).reshape(seq_len)
    pos_own = lax.dynamic_slice_in_dim(positions, ctx_here * rows_dev, rows_dev)
    doc_own = lax.dynamic_slice_in_dim(doc_slots, ctx_here * rows_dev, rows_dev)
    ids_own = lax.dynamic_slice_in_dim(block_ids, ctx_here * 2, 2)
    low_doc = doc_slots.reshape(blocks, sub)[:, 0]
    high_doc = doc_slots.reshape(blocks, sub)[:, -1]
    low_own = doc_own.reshape(2, sub)[:, 0]
    seen = (
        ((block_ids[None, :] <= ids_own[:, None]) & (high_doc[None, :] >= low_own[:, None]))
        .astype(jnp.int32)
        .reshape(2 * blocks)
    )
    marks = (
        pos_own.reshape(1, rows_dev), doc_own.reshape(1, rows_dev),
        positions.reshape(seq_len, 1), doc_slots.reshape(seq_len, 1),
    )
    cosine, sine = rotary_tables(pos_own)

    dp_bits, ctx_bits = bits_down("dp"), bits_down("ctx")
    core, far = ctx_bits[-1:], ctx_bits[:-1]
    near_x, along_z = dp_bits[-1:], dp_bits[:-1]
    kv_full = gather_rows(w_qkv[:, D:], dp_bits + ctx_bits)
    share = D // dp_size // ctx_size
    gains_here = jnp.pad(
        jnp.stack([gain_attn, gain_ffn]), ((0, 6), (0, D - D // dp_size))
    )
    q_part = jnp.concatenate(
        [lax.dynamic_slice_in_dim(w_qkv[:, :D], ctx_here * share, share), gains_here], 0
    )
    q_packed = gather(q_part, dp_bits + ctx_bits, along_z + far + near_x + core)
    q_packed = q_packed.reshape(dp_size, ctx_size, share + 8, D)
    q_full = q_packed[:, :, :share].reshape(D, D)
    gains = q_packed[:, 0, share : share + 2, : D // dp_size].astype(jnp.float32)
    gains = gains.transpose(1, 0, 2).reshape(2, D)
    in_full = gather_rows(w_in, dp_bits + core)
    out_rows_here = w_out.shape[0]
    tail = gather_rows(jnp.concatenate([w_out, w_down], 0), dp_bits + core)
    tail = tail.reshape(dp_size, -1, D)
    out_full = tail[:, :out_rows_here].reshape(D, D)
    down_full = tail[:, out_rows_here:].reshape(FF, D)
    x_rows = tokens[0].astype(jnp.float32)
    normed_attn, pull_attn = jax.vjp(layer_norm, x_rows, gains[0])
    normed_low = normed_attn.astype(jnp.bfloat16)
    kv_rows = jnp.dot(normed_low, kv_full, preferred_element_type=jnp.float32)
    keys_own = rotary(kv_rows[:, :D], cosine, sine).astype(jnp.bfloat16)
    kv_own = jnp.concatenate([keys_own, kv_rows[:, D:].astype(jnp.bfloat16)], 1)
    kv_all = gather(kv_own, ctx_bits, ctx_bits).reshape(seq_len, 2 * D)
    q_rows = jnp.dot(normed_low, q_full, preferred_element_type=jnp.float32)
    queries = (rotary(q_rows, cosine, sine) * score_scale).astype(jnp.bfloat16)
    attended_sum, log_total = attend(seen, queries, kv_all, marks)
    attended = attended_sum.astype(jnp.bfloat16)
    mid_rows = x_rows + jnp.dot(attended, out_full, preferred_element_type=jnp.float32)
    normed_ffn, pull_ffn = jax.vjp(layer_norm, mid_rows, gains[1])
    normed_second = normed_ffn.astype(jnp.bfloat16)
    gate_up = jnp.dot(normed_second, in_full, preferred_element_type=jnp.float32)
    mixed_float, pull_mix = jax.vjp(gated_gelu, gate_up[:, :FF], gate_up[:, FF:])
    mixed_low = mixed_float.astype(jnp.bfloat16)
    d_out_low = cotangent[0]
    d_mixed = contract(d_out_low, down_full, 1, 1)
    d_gate, d_up = pull_mix(d_mixed)
    d_gate_up = jnp.concatenate([d_gate, d_up], 1).astype(jnp.bfloat16)
    d_normed_second = contract(d_gate_up, in_full, 1, 1)
    d_mid_norm, grad_ffn_gain = pull_ffn(d_normed_second)
    d_mid = d_out_low.astype(jnp.float32) + d_mid_norm
    d_branch = d_mid.astype(jnp.bfloat16)
    grad_down = contract(mixed_low, d_out_low, 0, 0)
    grad_in = [contract(normed_second, d_gate_up[:, i * D : (i + 1) * D], 0, 0) for i in range(3)]
    grad_out = contract(attended, d_branch, 0, 0)
    in_parts = [by_owner(part) for part in grad_in]
    tail_parts = [by_owner(grad_down), by_owner(grad_out), gain_row(grad_ffn_gain)]
    in_packed = halve_all(pack_parts(in_parts), core)
    tail_packed = halve_all(pack_parts(tail_parts), core)
    d_att = contract(d_branch, out_full, 1, 1).astype(jnp.bfloat16)
    d_att, in_packed, tail_packed = lax.optimization_barrier((d_att, in_packed, tail_packed))
    in_packed = halve_all(in_packed, near_x)
    tail_packed = halve_all(tail_packed, far)
    d_queries, d_kv_all = pull_attend(seen, queries, kv_all, d_att, attended_sum, log_total, marks)
    out_rows = mid_rows + jnp.dot(mixed_low, down_full, preferred_element_type=jnp.float32)
    d_kv = d_kv_all.reshape((2,) + (2,) * len(ctx_bits) + (rows_dev, D))
    for step in core + far:
        d_kv = halve(d_kv, 1 + ctx_bits.index(step), step)
    d_kv, in_packed, tail_packed = lax.optimization_barrier((d_kv, in_packed, tail_packed))
    in_packed = halve_all(in_packed, along_z[::-1] + far)
    tail_packed = halve_all(tail_packed, near_x + along_z[::-1])
    in_sums = unpack_sums(in_packed, [part.shape[1] for part in in_parts])
    tail_sums = unpack_sums(tail_packed, [part.shape[1] for part in tail_parts])
    d_kv = d_kv.reshape(2, rows_dev, D)
    d_q = rotary(d_queries, cosine, -sine).astype(jnp.bfloat16)
    q_sums = owned_sums(
        [by_owner(contract(normed_low, d_q, 0, 0))], core + near_x + far + along_z[::-1]
    )
    d_v = d_kv[1]
    v_sums = owned_sums(
        [by_owner(contract(normed_low, d_v, 0, 0))], core + near_x + far + along_z[::-1]
    )
    d_k = rotary(d_kv[0].astype(jnp.float32), cosine, -sine).astype(jnp.bfloat16)
    d_normed_attn = contract(d_q, q_full, 1, 1) + contract(
        jnp.concatenate([d_k, d_v], 1), kv_full, 1, 1
    )
    d_x_norm, grad_attn_gain = pull_attn(d_normed_attn)
    grad_rows = (d_mid + d_x_norm).astype(jnp.bfloat16)
    k_sums = owned_sums(
        [by_owner(contract(normed_low, d_k, 0, 0)), gain_row(grad_attn_gain)],
        core + far + near_x + along_z[::-1],
    )
    return (
        out_rows.astype(jnp.bfloat16)[None],
        grad_rows[None],
        k_sums[1][0, : D // dp_size],
        tail_sums[2][0, : D // dp_size],
        jnp.concatenate([q_sums[0], k_sums[0], v_sums[0]], 1),
        tail_sums[1],
        jnp.concatenate(in_sums, 1),
        tail_sums[0],
    )


def solution(mesh):
    return jax.shard_map(
        on_device,
        mesh=mesh,
        in_specs=(
            P("dp", "ctx", None),
            P("dp", None),
            P(),
            P("dp"),
            P("dp"),
            P("dp", None),
            P("dp", None),
            P("dp", None),
            P("dp", None),
            P("dp", "ctx", None),
        ),
        out_specs=(
            P("dp", "ctx", None),
            P("dp", "ctx", None),
            P("dp"),
            P("dp"),
            P("dp", None),
            P("dp", None),
            P("dp", None),
            P("dp", None),
        ),
        check_vma=False,
    )
```
